32 devices in a mesh: grp: 4 (over y, x), sub: 8 (over z, core).
Axes of the slice: x: 2, y: 2, z: 4, core: 2. Of those that a mesh axis runs over, the one named last changes fastest.
Arguments:
- neumann: bfloat16 [4, 8, 1024, 1024], P('grp', 'sub'), may hold values from -1 to 4
- dirichlet: bfloat16 [4, 8, 1024, 1024], P('grp', 'sub'), may hold values from -1 to 4
- coarse_inverse: float32 [4, 8, 128, 256], P('grp', 'sub'), may hold values from -1 to 3
- loads: bfloat16 [4, 8, 1024, 256], P('grp', 'sub'), may hold values from -72 to 72
- iface_sizes: int32 [4, 8], P('grp', 'sub'), may hold values from 1 to 512, 2048 in all within a row
- wave_dirs: int32 [4, 8, 32], P('grp', 'sub'), may hold values from 0 to 63
Outputs:
- dual: float32 [4, 8, 512, 256], P('grp', 'sub')
- residual: float32 [4, 8, 512, 256], P('grp', 'sub')
The draws below stay inside these ranges and needn't reach their ends.
Inputs may be any that keep to these rules, and one draw needn't show every extreme that they name: `iface_sizes`: the 8 sizes of one group sum to 2048, and in each group one size is exactly 512.
All inputs are finite; a program needn't handle non-finite values.
Results may differ from the reference program's by a relative error of at most 0.005.
Values may be sent and summed in bfloat16 or wider, within the bound.
A program may use at most 64 MiB of HBM per device.

```python
import math
import jax
import jax.numpy as jnp
import numpy as np
from jax import lax

NB = 1024
WAVES = 32
NDIR = 64
RHS = 256
ITERS = 2
KMAX = 512
N_GRP = 4
N_SUB = 8


def schur_draw(key, low, high):
    keys = jax.random.split(key, N_GRP * N_SUB)

    def single(one_key):
        noise_key, diag_key = jax.random.split(one_key)
        noise = jnp.clip(jax.random.normal(noise_key, (NB, NB), jnp.float32), -5.0, 5.0)
        symmetric = (noise + noise.T) * (0.6 / jnp.sqrt(2.0 * NB))
        diagonal = jax.random.uniform(diag_key, (NB,), jnp.float32, low, high)
        return (symmetric + jnp.diag(diagonal)).astype(jnp.bfloat16)
    return lax.map(single, keys).reshape(N_GRP, N_SUB, NB, NB)


def draw_neumann(key, part):
    return schur_draw(jax.random.fold_in(key, 11), 1.5, 3.0)


def draw_dirichlet(key, part):
    return schur_draw(jax.random.fold_in(key, 23), 1.5, 3.0)


def draw_coarse_inverse(key, part):
    total_rows = N_GRP * WAVES
    total_cols = N_SUB * WAVES
    count = N_GRP * N_SUB
    keys = jax.random.split(jax.random.fold_in(key, 37), count)
    factor = 0.8 / jnp.sqrt(1.0 * N_GRP * N_SUB * WAVES)

    def single(pair):
        index, one_key = pair
        noise_key, diag_key = jax.random.split(one_key)
        noise = jnp.clip(jax.random.normal(noise_key, (total_rows, total_cols), jnp.float32), -5.0, 5.0)
        group = index // N_SUB
        member = index % N_SUB
        row_ids = jnp.arange(total_rows)[:, None]
        col_ids = jnp.arange(total_cols)[None, :]
        on_diag = (row_ids // WAVES == group) & (col_ids // WAVES == member) & (row_ids % WAVES == col_ids % WAVES)
        diagonal = jax.random.uniform(diag_key, (total_rows, total_cols), jnp.float32, 1.0, 2.0)
        return noise * factor + jnp.where(on_diag, diagonal, 0.0)
    tiles = lax.map(single, (jnp.arange(count), keys))
    return tiles.reshape(N_GRP, N_SUB, total_rows, total_cols)


def draw_loads(key, part):
    keys = jax.random.split(jax.random.fold_in(key, 53), 3)
    shape = (N_GRP, N_SUB, NB, RHS)
    place = jnp.arange(N_GRP * N_SUB).astype(jnp.float32).reshape(N_GRP, N_SUB, 1, 1) / (N_GRP * N_SUB - 1)
    noise = jnp.clip(jax.random.normal(keys[0], shape, jnp.float32), -4.0, 4.0)
    ramp = 1.0 + place
    row_scale = jnp.exp(jax.random.uniform(keys[1], (N_GRP, N_SUB, NB, 1), jnp.float32, jnp.log(0.3), jnp.log(3.0)))
    col_scale = jnp.exp(jax.random.uniform(keys[2], (1, 1, 1, RHS), jnp.float32, jnp.log(0.5), jnp.log(2.0)))
    return (noise * row_scale * col_scale * ramp).astype(jnp.bfloat16)


def plant(result, own_key, low, top_value):
    spot = [jax.random.randint(jax.random.fold_in(own_key, axis), (), 0, length) for axis, length in enumerate(result.shape)]
    main_axis = result.shape.index(max(result.shape))
    neighbour = spot[:main_axis] + [(spot[main_axis] + 1) % result.shape[main_axis]] + spot[main_axis + 1:]
    return result.at[tuple(spot)].set(low).at[tuple(neighbour)].set(top_value)


def profile(number_of, total, most, skew):
    portions = [(1 << 20) // math.isqrt(rank ** skew) + 1 for rank in range(2, number_of + 1)]
    surplus, counts = total - most - (number_of - 1), [1] * (number_of - 1)
    while surplus > 0:
        movable = [i for i in range(number_of - 1) if counts[i] < most]
        whole, remaining = sum([portions[i] for i in movable]), surplus
        for i in movable:
            extra = min(most - counts[i], max(1, remaining * portions[i] // whole), surplus)
            counts[i] = counts[i] + extra
            surplus = surplus - extra
    return np.array([most] + counts)


def ragged(own_key, count, total, bound, skew):
    if count == 2:
        one = jax.random.randint(own_key, (), max(1, total - bound), min(bound, total - 1) + 1)
        return jnp.stack([one, total - one])
    lengths = jnp.asarray(profile(count, total, bound, skew), jnp.int32)
    couples = (count - 1) // 2
    source_of, receiver = lengths[1:1 + 2 * couples:2], lengths[2:2 + 2 * couples:2]
    slack = jnp.minimum(source_of - 1, bound - receiver)
    shifted = jax.random.randint(jax.random.fold_in(own_key, 1), (couples,), 0, 1 << 20) % (slack + 1)
    lengths = lengths.at[1:1 + 2 * couples:2].set(source_of - shifted).at[2:2 + 2 * couples:2].set(receiver + shifted)
    return lengths[jax.random.permutation(jax.random.fold_in(own_key, 2), count)]


def setup_inputs(seed: int = 0) -> dict:
    seeds = jax.random.split(jax.random.key(seed), 7)
    return {
        "neumann": draw_neumann(jax.random.fold_in(seeds[6], 71), 0),
        "dirichlet": draw_dirichlet(jax.random.fold_in(seeds[6], 71), 0),
        "coarse_inverse": draw_coarse_inverse(jax.random.fold_in(seeds[6], 71), 0),
        "loads": draw_loads(jax.random.fold_in(seeds[6], 71), 0),
        "iface_sizes": jax.vmap(lambda own: ragged(own, N_SUB, N_SUB * KMAX // 2, KMAX, 2))(jax.random.split(seeds[4], N_GRP)).reshape((N_GRP, N_SUB)).astype(jnp.int32),
        "wave_dirs": plant(jax.random.randint(seeds[5], (N_GRP, N_SUB, WAVES), 0, NDIR), jax.random.fold_in(seeds[5], 1), 0, NDIR - 1).astype(jnp.int32),
    }


wave_number = 0.785
highest = lax.Precision.HIGHEST

def make_waves(iface_sizes, wave_dirs):
    rows = jnp.arange(KMAX).astype(jnp.float32)
    live = (jnp.arange(KMAX)[None, None, :] < iface_sizes[:, :, None]).astype(jnp.float32)
    angle = 2.0 * jnp.pi * wave_dirs.astype(jnp.float32) / NDIR
    phase = (jnp.arange(WAVES) % 2).astype(jnp.float32) * (jnp.pi / 2.0)
    basis = jnp.cos(wave_number * rows[None, None, :, None] * jnp.cos(angle)[:, :, None, :] + phase)
    return (basis * live[..., None] / jnp.sqrt(jnp.float32(KMAX)), live)

def spread(values):
    left = jnp.roll(values, 1, axis=1)
    middle = jnp.zeros((N_GRP, N_SUB, NB - 2 * KMAX, RHS), jnp.bfloat16)
    return jnp.concatenate([-left, middle, jnp.flip(values, 2)], axis=2)

def product_ends(mats, vectors):

    def single(pair):
        product = jnp.dot(pair[0], pair[1], preferred_element_type=jnp.float32)
        return (product[:KMAX], product[NB - KMAX:])
    heads, tails = lax.map(single, (mats.reshape(-1, NB, NB), vectors.reshape(-1, NB, RHS)))
    return (heads.reshape(N_GRP, N_SUB, KMAX, RHS), tails.reshape(N_GRP, N_SUB, KMAX, RHS))

def jump(heads, tails, live):
    return (jnp.flip(tails, 2) - jnp.roll(heads, -1, axis=1)) * live[..., None]

def apply_op(mats, values, live):
    heads, tails = product_ends(mats, spread(values.astype(jnp.bfloat16)))
    return jump(heads, tails, live)

def correct(values, basis, tiles):
    coef = jnp.einsum('gskm,gskr->gsmr', basis, values, precision=highest)
    whole = coef.reshape(N_GRP, N_SUB * WAVES, RHS)
    terms = jnp.einsum('gsac,gcr->gsar', tiles, whole, precision=highest)
    summed = terms.reshape(N_GRP, N_SUB, N_GRP, WAVES, RHS).sum(axis=0)
    summed = jnp.transpose(summed, (1, 0, 2, 3))
    return jnp.einsum('gskm,gsmr->gskr', basis, summed, precision=highest)

def reference(neumann, dirichlet, coarse_inverse, loads, iface_sizes, wave_dirs):
    basis, live = make_waves(iface_sizes, wave_dirs)
    heads, tails = product_ends(neumann, loads)
    dual_rhs = jump(heads, tails, live)
    dual = correct(dual_rhs, basis, coarse_inverse)
    residual = dual_rhs - apply_op(neumann, dual, live)
    direction = dual_rhs
    rho_prev = jnp.ones((RHS,), jnp.float32)
    for step in range(ITERS):
        projected = residual - correct(residual, basis, coarse_inverse)
        precond = apply_op(dirichlet, projected, live)
        rho = lax.optimization_barrier(jnp.sum(projected * precond, axis=(0, 1, 2)))
        search = precond - correct(precond, basis, coarse_inverse)
        if step == 0:
            direction = search
        else:
            direction = search + rho / rho_prev * direction
        image = apply_op(neumann, direction, live)
        alpha = rho / lax.optimization_barrier(jnp.sum(direction * image, axis=(0, 1, 2)))
        dual = dual + alpha * direction
        residual = residual - alpha * image
        rho_prev = rho
    return (dual, residual)
```

```python
import functools

import jax
import jax.numpy as jnp
from jax import lax
from jax.experimental import pallas as pl
from jax.experimental.pallas import tpu as pltpu
from jax.sharding import PartitionSpec as P

NDIR = 64
ITERS = 2
WAVE_NUMBER = 0.785
STAT = 8
MESH = pl.DeviceIdType.MESH
f32, bf16 = jnp.float32, jnp.bfloat16


def dot(a, b):
    return jnp.dot(a, b, preferred_element_type=f32)


def split(values):
    high = values.astype(bf16)
    return high, (values - high.astype(f32)).astype(bf16)


def kernel(
    groups, members, size_ref, dirs_ref, neumann, dirichlet_hbm, loads, tile,
    dual_ref, res_ref,
    dirichlet, n_left, n_right, d_left, d_right, n_send, d_send,
    u_send, u_recv, tile_nb, tile_hi, tile_lo, bases, wave_cat, wave_t,
    gath, stage, red, r_send, r_recv,
    res3, dir3, vec, x_left, x_right,
    load_sem, set_send, set_recv, g_send, f_send, g_recv, red_send, red_recv, r_ssem, r_rsem,
):
    reach = n_left.shape[0]
    columns = loads.shape[1]
    waves = dirs_ref.shape[1]
    span = 3 * waves
    half = members // 2
    g, s = lax.axis_index("grp"), lax.axis_index("sub")
    nxt, prv = lax.rem(s + 1, members), lax.rem(s + members - 1, members)
    partner = s + 1 - 2 * lax.rem(s, 2)

    def remote(src, dst, send, recv, to):
        return pltpu.make_async_remote_copy(
            src_ref=src, dst_ref=dst, send_sem=send, recv_sem=recv, device_id=to, device_id_type=MESH
        )

    load_d = pltpu.make_async_copy(dirichlet_hbm, dirichlet, load_sem)
    load_d.start()

    barrier = pltpu.get_barrier_semaphore()

    def greet_sub(k, carry):
        pl.semaphore_signal(barrier, inc=1, device_id=(g, lax.rem(s + k, members)), device_id_type=MESH)
        return carry

    lax.fori_loop(1, members, greet_sub, 0)
    for k in range(1, groups):
        pl.semaphore_signal(barrier, inc=1, device_id=(lax.rem(g + k, groups), s), device_id_type=MESH)

    u_send[...] = dot(neumann[:reach, :], loads[...])
    pl.semaphore_wait(barrier, members - 1 + groups - 1)
    send_u = remote(u_send, u_recv, set_send.at[0], set_recv.at[0], (g, prv))
    send_u.start()
    send_t = [
        remote(tile, tile_nb.at[0], set_send.at[1], set_recv.at[1], (g, nxt)),
        remote(tile, tile_nb.at[1], set_send.at[2], set_recv.at[2], (g, prv)),
    ]

    back = (
        lax.broadcasted_iota(jnp.int32, (reach, reach), 0) + lax.broadcasted_iota(jnp.int32, (reach, reach), 1)
        == reach - 1
    )
    flip = jnp.where(back, 1.0, 0.0).astype(bf16)

    def prepare(matrix, left, outgoing):
        outgoing[:, :reach] = matrix[:reach, :reach]
        outgoing[:, reach:] = dot(matrix[:reach, reach:], flip).astype(bf16)
        left[...] = dot(flip, matrix[reach:, :]).astype(bf16)

    prepare(neumann, n_left, n_send)
    v = dot(n_left[...], loads[...])
    vec[...] = v
    n_left[:, reach:] = dot(n_left[:, reach:], flip).astype(bf16)

    size = size_ref[0, 0]
    rows = lax.broadcasted_iota(jnp.int32, (waves, reach), 1)
    same = (
        lax.broadcasted_iota(jnp.int32, (waves, waves), 0) == lax.broadcasted_iota(jnp.int32, (waves, waves), 1)
    )
    dirs = jnp.sum(jnp.where(same, dirs_ref[...].astype(f32), 0.0), axis=1, keepdims=True)
    angle = 2.0 * jnp.pi * dirs / NDIR
    odd = lax.rem(lax.broadcasted_iota(jnp.int32, (waves, 1), 0), 2).astype(f32)
    basis = jnp.cos(WAVE_NUMBER * rows.astype(f32) * jnp.cos(angle) + odd * (jnp.pi / 2.0))
    basis = jnp.where(rows < size, basis, 0.0) / jnp.sqrt(f32(reach))
    high, low = split(basis)
    wave_t[:waves, :] = high
    wave_t[waves:, :] = low
    bases[1] = basis

    def stack_waves(k):
        hi, lo = split(bases[k])
        fill = jnp.zeros((wave_cat.shape[2] - span, reach), f32)
        padded = jnp.concatenate([hi.astype(f32), lo.astype(f32), hi.astype(f32), fill], axis=0)
        wave_cat[k] = padded.T.astype(bf16)

    send_w = [
        remote(bases.at[1], bases.at[0], set_send.at[3], set_recv.at[3], (g, nxt)),
        remote(bases.at[1], bases.at[2], set_send.at[4], set_recv.at[4], (g, prv)),
    ]
    send_n = remote(n_send, n_right, set_send.at[5], set_recv.at[5], (g, prv))
    send_d = remote(d_send, d_right, set_send.at[6], set_recv.at[6], (g, prv))
    send_u.wait_send()
    for copy in send_t + send_w + [send_n]:
        copy.start()

    live = lax.broadcasted_iota(jnp.int32, (reach, columns), 0) < size
    send_u.wait_recv()
    rhs = jnp.where(live, vec[...] - u_recv[...], 0.0)
    res3[1] = rhs

    def lift(k, coarse):
        hi, lo = split(coarse)
        fill = jnp.zeros((wave_cat.shape[2] - span, columns), bf16)
        return dot(wave_cat[k], jnp.concatenate([hi, hi, lo, fill], axis=0))

    def product(left, right):
        return jnp.where(live, dot(left[...], x_left[...]) + dot(right[...], x_right[...]), 0.0)

    def set_x(k, values):
        if k == 0:
            x_left[:reach, :] = (-values).astype(bf16)
        elif k == 1:
            own = values.astype(bf16)
            x_left[reach:, :] = own
            x_right[:reach, :] = own
        else:
            x_right[reach:, :] = (-values).astype(bf16)

    def fold(values):
        return jnp.sum(values.reshape(reach // STAT, STAT, columns), axis=0)

    def exchange(slot, lo, count, hook=None):
        part = pl.ds(lo, count)

        def block(owner):
            return gath.at[slot, owner, part]

        def send_peer(k):
            to = lax.rem(s + 2 * k, members)
            return remote(block(s), block(s), g_send.at[slot, k], g_recv.at[slot, s], (g, to))

        def relay(k):
            src = lax.rem(s + members - 2 * k, members)
            return remote(block(src), block(src), f_send.at[slot, k], g_recv.at[slot, src], (g, partner))

        def arrival(k):
            src = lax.rem(partner + members - 2 * k, members)
            return remote(block(src), block(src), f_send.at[slot, k], g_recv.at[slot, src], (g, partner))

        def loop(low, body):
            def step(k, carry):
                body(k)
                return carry

            lax.fori_loop(low, half, step, 0, unroll=half <= 8)

        loop(1, lambda k: send_peer(k).start())
        relay(0).start()
        if hook is not None:
            hook()

        def pass_on(k):
            relay(k).wait_recv()
            relay(k).start()

        loop(1, pass_on)
        loop(0, lambda k: arrival(k).wait_recv())
        loop(1, lambda k: send_peer(k).wait_send())
        loop(0, lambda k: relay(k).wait_send())

    def reduce_groups(slot, lo, count):
        part = pl.ds(lo, count)

        def to_group(k):
            h = lax.rem(g + k, groups)
            return remote(
                stage.at[h, part], red.at[slot, g, part], red_send.at[slot, k], red_recv.at[slot, g], (h, s)
            )

        def from_group(k):
            h = lax.rem(g + groups - k, groups)
            return remote(
                stage.at[h, part], red.at[slot, h, part], red_send.at[slot, k], red_recv.at[slot, h], (h, s)
            )

        for k in range(1, groups):
            to_group(k).start()
        red[slot, g, part] = stage[g, part]
        for k in range(1, groups):
            from_group(k).wait_recv()
        for k in range(1, groups):
            to_group(k).wait_send()
        return jnp.sum(red[slot, :, part, :], axis=0)

    def send_rows(slot):
        return [
            remote(r_send.at[slot], r_recv.at[slot, 0], r_ssem.at[slot, 0], r_rsem.at[slot, 0], (g, nxt)),
            remote(r_send.at[slot], r_recv.at[slot, 1], r_ssem.at[slot, 1], r_rsem.at[slot, 1], (g, prv)),
        ]

    def coarse_round(slot, values, stat, share, hook=None):
        hi, lo = split(values)
        both = dot(wave_t[...], hi)
        gath[slot, s, :waves, :] = both[:waves] + both[waves:] + dot(wave_t[:waves, :], lo)
        gath[slot, s, waves:, :] = jnp.zeros((STAT, columns), f32) if stat is None else stat
        if share:
            r_send[slot] = hi

        exchange(slot, 0, waves + STAT, hook)
        if share:
            for copy in send_rows(slot):
                copy.start()
        blocks = gath[slot]
        c_hi, c_lo = split(blocks[:, :waves, :].reshape(members * waves, columns))
        terms = dot(tile_hi[...], c_hi) + dot(tile_lo[...], c_hi) + dot(tile_hi[...], c_lo)
        group_stat = jnp.sum(blocks[:, waves:, :], axis=0)
        for h in range(groups):
            stage[h, :span, :] = terms[h * span : (h + 1) * span]
            stage[h, span:, :] = group_stat
        total = reduce_groups(slot, 0, span + STAT)
        if share:
            for copy in send_rows(slot):
                copy.wait()
        coarse = [total[k * waves : (k + 1) * waves] for k in range(3)]
        return coarse, jnp.sum(total[span:], axis=0, keepdims=True)

    def first_hook():
        for copy in send_t:
            copy.wait()
        for h in range(groups):
            for k, source in enumerate((tile_nb.at[0], tile, tile_nb.at[1])):
                hi, lo = split(source[h * waves : (h + 1) * waves, :])
                tile_hi[h * span + k * waves : h * span + (k + 1) * waves, :] = hi
                tile_lo[h * span + k * waves : h * span + (k + 1) * waves, :] = lo
        load_d.wait()
        prepare(dirichlet, d_left, d_send)
        d_left[:, reach:] = dot(d_left[:, reach:], flip).astype(bf16)
        for copy in send_w:
            copy.wait()
        for k in range(3):
            stack_waves(k)

    coarse, _ = coarse_round(0, rhs, None, False, first_hook)
    for k in range(3):
        lifted = lift(k, coarse[k])
        set_x(k, lifted)
        if k == 1:
            dual_ref[...] = lifted
    send_n.wait()
    send_d.start()
    residual = res3[1] - product(n_left, n_right)
    res3[1] = residual

    coarse_res, _ = coarse_round(1, residual, None, True)
    res3[0] = r_recv[1, 0].astype(f32)
    res3[2] = r_recv[1, 1].astype(f32)
    rho_prev = None
    slot = 0
    for step in range(ITERS):
        for k in range(3):
            projected = res3[k] - lift(k, coarse_res[k])
            set_x(k, projected)
            if k == 1:
                vec[...] = projected
        if step == 0:
            send_d.wait()
        precond = product(d_left, d_right)
        coarse, rho = coarse_round(slot, precond, fold(vec[...] * precond), True)
        vec[...] = precond
        for k in range(3):
            own = vec[...] if k == 1 else r_recv[slot, k // 2].astype(f32)
            direction = own - lift(k, coarse[k])
            if step > 0:
                direction = direction + rho / rho_prev * dir3[k]
            dir3[k] = direction
            set_x(k, direction)
        slot = 1 - slot
        image = product(n_left, n_right)
        vec[...] = image
        stat = fold(dir3[1] * image)
        if step + 1 < ITERS:
            coarse, curvature = coarse_round(slot, image, stat, True)
            alpha = rho / curvature
            coarse_res = [old - alpha * new for old, new in zip(coarse_res, coarse)]
            res3[0] = res3[0] - alpha * r_recv[slot, 0].astype(f32)
            res3[2] = res3[2] - alpha * r_recv[slot, 1].astype(f32)
            res3[1] = res3[1] - alpha * vec[...]
            dual_ref[...] = dual_ref[...] + alpha * dir3[1]
        else:
            gath[slot, s, waves:, :] = stat
            exchange(slot, waves, STAT)
            group_stat = jnp.sum(gath[slot, :, waves:, :], axis=0)
            for h in range(groups):
                stage[h, span:, :] = group_stat
            alpha = rho / jnp.sum(reduce_groups(slot, span, STAT), axis=0, keepdims=True)
            dual_ref[...] = dual_ref[...] + alpha * dir3[1]
            res_ref[...] = res3[1] - alpha * vec[...]
        slot = 1 - slot
        rho_prev = rho


def shards(neumann, dirichlet, coarse_inverse, loads, iface_sizes, wave_dirs):
    width = neumann.shape[2]
    reach = width // 2
    columns = loads.shape[3]
    waves = wave_dirs.shape[2]
    groups, members = lax.axis_size("grp"), lax.axis_size("sub")
    rows, depth = coarse_inverse.shape[2:]
    span = 3 * waves
    vmem = pl.BlockSpec(memory_space=pltpu.VMEM)
    dma = pltpu.SemaphoreType.DMA
    vector = jax.ShapeDtypeStruct((reach, columns), f32)
    half_matrix = pltpu.VMEM((reach, width), bf16)
    dual, residual = pl.pallas_call(
        functools.partial(kernel, groups, members),
        out_shape=(vector, vector),
        in_specs=[
            pl.BlockSpec(memory_space=pltpu.SMEM), vmem, vmem, pl.BlockSpec(memory_space=pl.ANY), vmem, vmem,
        ],
        out_specs=(vmem, vmem),
        scratch_shapes=[
            pltpu.VMEM((width, width), bf16),
            half_matrix, half_matrix, half_matrix, half_matrix, half_matrix, half_matrix,
            pltpu.VMEM((reach, columns), f32),
            pltpu.VMEM((reach, columns), f32),
            pltpu.VMEM((2, rows, depth), f32),
            pltpu.VMEM((groups * span, depth), bf16),
            pltpu.VMEM((groups * span, depth), bf16),
            pltpu.VMEM((3, waves, reach), f32),
            pltpu.VMEM((3, reach, pl.cdiv(span, 128) * 128), bf16),
            pltpu.VMEM((2 * waves, reach), bf16),
            pltpu.VMEM((2, members, waves + STAT, columns), f32),
            pltpu.VMEM((groups, span + STAT, columns), f32),
            pltpu.VMEM((2, groups, span + STAT, columns), f32),
            pltpu.VMEM((2, reach, columns), bf16),
            pltpu.VMEM((2, 2, reach, columns), bf16),
            pltpu.VMEM((3, reach, columns), f32),
            pltpu.VMEM((3, reach, columns), f32),
            pltpu.VMEM((reach, columns), f32),
            pltpu.VMEM((width, columns), bf16),
            pltpu.VMEM((width, columns), bf16),
            dma,
            dma((7,)),
            dma((7,)),
            dma((2, members // 2)),
            dma((2, members // 2)),
            dma((2, members)),
            dma((2, groups)),
            dma((2, groups)),
            dma((2, 2)),
            dma((2, 2)),
        ],
        compiler_params=pltpu.CompilerParams(
            collective_id=0, has_side_effects=True, vmem_limit_bytes=56 * 1024 * 1024
        ),
        cost_estimate=pl.CostEstimate(
            flops=14 * width * width * columns, bytes_accessed=5 * width * width, transcendentals=0
        ),
        name="dual_iterations",
    )(iface_sizes, wave_dirs[0], neumann[0, 0], dirichlet[0, 0], loads[0, 0], coarse_inverse[0, 0])
    return (dual[None, None], residual[None, None])


def solution(mesh):
    return jax.shard_map(
        shards,
        mesh=mesh,
        in_specs=(
            P("grp", "sub", None, None),
            P("grp", "sub", None, None),
            P("grp", "sub", None, None),
            P("grp", "sub", None, None),
            P("grp", "sub"),
            P("grp", "sub", None),
        ),
        out_specs=(P("grp", "sub", None, None), P("grp", "sub", None, None)),
        check_vma=False,
    )
```

```python
import functools

import jax
import jax.numpy as jnp
from jax import lax
from jax.experimental import pallas as pl
from jax.experimental.pallas import tpu as pltpu
from jax.sharding import PartitionSpec as P

NDIR = 64
ITERS = 2
WAVE_NUMBER = 0.785
STAT = 8
PIPES = 2
MESH = pl.DeviceIdType.MESH
f32, bf16 = jnp.float32, jnp.bfloat16


def dot(a, b):
    return jnp.dot(a, b, preferred_element_type=f32)


def split(values):
    high = values.astype(bf16)
    return high, (values - high.astype(f32)).astype(bf16)


def kernel(
    groups, members, size_ref, dirs_ref, neumann, dirichlet_hbm, loads, tile,
    dual_ref, res_ref,
    dirichlet, n_left, n_right, d_left, d_right, n_send, d_send,
    u_send, u_recv, tile_nb, tile_hi, tile_lo, bases, wave_cat, wave_t,
    gath, stage, red, r_send, r_recv,
    res3, dir3, vec, first, x_left, x_right,
    load_sem, set_send, set_recv, g_send, f_send, g_recv, red_send, red_recv, r_ssem, r_rsem,
):
    reach = n_left.shape[0]
    columns = loads.shape[1]
    waves = dirs_ref.shape[1]
    span = 3 * waves
    half = members // 2
    g, s = lax.axis_index("grp"), lax.axis_index("sub")
    nxt, prv = lax.rem(s + 1, members), lax.rem(s + members - 1, members)
    partner = s + 1 - 2 * lax.rem(s, 2)

    def remote(src, dst, send, recv, to):
        return pltpu.make_async_remote_copy(
            src_ref=src, dst_ref=dst, send_sem=send, recv_sem=recv, device_id=to, device_id_type=MESH
        )

    load_d = pltpu.make_async_copy(dirichlet_hbm, dirichlet, load_sem)
    load_d.start()

    barrier = pltpu.get_barrier_semaphore()

    def greet_sub(k, carry):
        pl.semaphore_signal(barrier, inc=1, device_id=(g, lax.rem(s + k, members)), device_id_type=MESH)
        return carry

    lax.fori_loop(1, members, greet_sub, 0)
    for k in range(1, groups):
        pl.semaphore_signal(barrier, inc=1, device_id=(lax.rem(g + k, groups), s), device_id_type=MESH)

    u_send[...] = dot(neumann[:reach, :], loads[...])
    pl.semaphore_wait(barrier, members - 1 + groups - 1)
    send_u = remote(u_send, u_recv, set_send.at[0], set_recv.at[0], (g, prv))
    send_u.start()
    send_t = [
        remote(tile, tile_nb.at[0], set_send.at[1], set_recv.at[1], (g, nxt)),
        remote(tile, tile_nb.at[1], set_send.at[2], set_recv.at[2], (g, prv)),
    ]

    back = (
        lax.broadcasted_iota(jnp.int32, (reach, reach), 0) + lax.broadcasted_iota(jnp.int32, (reach, reach), 1)
        == reach - 1
    )
    flip = jnp.where(back, 1.0, 0.0).astype(bf16)

    def prepare(matrix, left, outgoing):
        outgoing[:, :reach] = matrix[:reach, :reach]
        outgoing[:, reach:] = dot(matrix[:reach, reach:], flip).astype(bf16)
        left[...] = dot(flip, matrix[reach:, :]).astype(bf16)

    prepare(neumann, n_left, n_send)
    v = dot(n_left[...], loads[...])
    first[...] = v
    n_left[:, reach:] = dot(n_left[:, reach:], flip).astype(bf16)

    size = size_ref[0, 0]
    rows = lax.broadcasted_iota(jnp.int32, (waves, reach), 1)
    same = (
        lax.broadcasted_iota(jnp.int32, (waves, waves), 0) == lax.broadcasted_iota(jnp.int32, (waves, waves), 1)
    )
    dirs = jnp.sum(jnp.where(same, dirs_ref[...].astype(f32), 0.0), axis=1, keepdims=True)
    angle = 2.0 * jnp.pi * dirs / NDIR
    odd = lax.rem(lax.broadcasted_iota(jnp.int32, (waves, 1), 0), 2).astype(f32)
    basis = jnp.cos(WAVE_NUMBER * rows.astype(f32) * jnp.cos(angle) + odd * (jnp.pi / 2.0))
    basis = jnp.where(rows < size, basis, 0.0) / jnp.sqrt(f32(reach))
    high, low = split(basis)
    wave_t[:waves, :] = high
    wave_t[waves:, :] = low
    bases[1] = basis

    def stack_waves(k):
        hi, lo = split(bases[k])
        fill = jnp.zeros((wave_cat.shape[2] - span, reach), f32)
        padded = jnp.concatenate([hi.astype(f32), lo.astype(f32), hi.astype(f32), fill], axis=0)
        wave_cat[k] = padded.T.astype(bf16)

    send_w = [
        remote(bases.at[1], bases.at[0], set_send.at[3], set_recv.at[3], (g, nxt)),
        remote(bases.at[1], bases.at[2], set_send.at[4], set_recv.at[4], (g, prv)),
    ]
    send_n = remote(n_send, n_right, set_send.at[5], set_recv.at[5], (g, prv))
    send_d = remote(d_send, d_right, set_send.at[6], set_recv.at[6], (g, prv))
    send_u.wait_send()
    for copy in send_t + send_w + [send_n]:
        copy.start()

    cols = columns // PIPES
    live = lax.broadcasted_iota(jnp.int32, (reach, cols), 0) < size

    def lift(k, coarse):
        hi, lo = split(coarse)
        fill = jnp.zeros((wave_cat.shape[2] - span, cols), bf16)
        return dot(wave_cat[k], jnp.concatenate([hi, hi, lo, fill], axis=0))

    def fold(values):
        return jnp.sum(values.reshape(reach // STAT, STAT, cols), axis=0)

    def loop(low, body):
        def step(k, carry):
            body(k)
            return carry

        lax.fori_loop(low, half, step, 0, unroll=half <= 8)

    def pipeline(p):
        part_cols = slice(p * cols, (p + 1) * cols)

        def product(left, right):
            return jnp.where(live, dot(left[...], x_left[p]) + dot(right[...], x_right[p]), 0.0)

        def set_x(k, values):
            if k == 0:
                x_left[p, :reach, :] = (-values).astype(bf16)
            elif k == 1:
                own = values.astype(bf16)
                x_left[p, reach:, :] = own
                x_right[p, :reach, :] = own
            else:
                x_right[p, reach:, :] = (-values).astype(bf16)

        def exchange(slot, lo, count):
            part = pl.ds(lo, count)

            def block(owner):
                return gath.at[p, slot, owner, part]

            def send_peer(k):
                to = lax.rem(s + 2 * k, members)
                return remote(block(s), block(s), g_send.at[p, slot, k], g_recv.at[p, slot, s], (g, to))

            def relay(k):
                src = lax.rem(s + members - 2 * k, members)
                return remote(block(src), block(src), f_send.at[p, slot, k], g_recv.at[p, slot, src], (g, partner))

            def arrival(k):
                src = lax.rem(partner + members - 2 * k, members)
                return remote(block(src), block(src), f_send.at[p, slot, k], g_recv.at[p, slot, src], (g, partner))

            loop(1, lambda k: send_peer(k).start())
            relay(0).start()
            yield

            def pass_on(k):
                relay(k).wait_recv()
                relay(k).start()

            loop(1, pass_on)
            loop(0, lambda k: arrival(k).wait_recv())
            loop(1, lambda k: send_peer(k).wait_send())
            loop(0, lambda k: relay(k).wait_send())

        def reduce_groups(slot, lo, count):
            part = pl.ds(lo, count)

            def message(k, h, origin):
                return remote(
                    stage.at[p, h, part], red.at[p, slot, origin, part],
                    red_send.at[p, slot, k], red_recv.at[p, slot, origin], (h, s),
                )

            out = [message(k, lax.rem(g + k, groups), g) for k in range(1, groups)]
            into = [lax.rem(g + groups - k, groups) for k in range(1, groups)]
            for copy in out:
                copy.start()
            red[p, slot, g, part] = stage[p, g, part]
            yield
            for k, h in enumerate(into):
                message(k + 1, h, h).wait_recv()
            for copy in out:
                copy.wait_send()
            return jnp.sum(red[p, slot, :, part, :], axis=0)

        def send_rows(slot):
            return [
                remote(r_send.at[p, slot], r_recv.at[p, slot, side], r_ssem.at[p, slot, side],
                       r_rsem.at[p, slot, side], (g, to))
                for side, to in enumerate((nxt, prv))
            ]

        def coarse_round(slot, values, stat, share):
            hi, lo = split(values)
            both = dot(wave_t[...], hi)
            gath[p, slot, s, :waves, :] = both[:waves] + both[waves:] + dot(wave_t[:waves, :], lo)
            gath[p, slot, s, waves:, :] = jnp.zeros((STAT, cols), f32) if stat is None else stat
            if share:
                r_send[p, slot] = hi
            yield from exchange(slot, 0, waves + STAT)
            if share:
                for copy in send_rows(slot):
                    copy.start()
            blocks = gath[p, slot]
            c_hi, c_lo = split(blocks[:, :waves, :].reshape(members * waves, cols))
            terms = dot(tile_hi[...], c_hi) + dot(tile_lo[...], c_hi) + dot(tile_hi[...], c_lo)
            group_stat = jnp.sum(blocks[:, waves:, :], axis=0)
            for h in range(groups):
                stage[p, h, :span, :] = terms[h * span : (h + 1) * span]
                stage[p, h, span:, :] = group_stat
            total = yield from reduce_groups(slot, 0, span + STAT)
            if share:
                for copy in send_rows(slot):
                    copy.wait()
            coarse = [total[k * waves : (k + 1) * waves] for k in range(3)]
            return coarse, jnp.sum(total[span:], axis=0, keepdims=True)

        rhs = jnp.where(live, first[:, part_cols] - u_recv[:, part_cols], 0.0)
        res3[p, 1] = rhs
        coarse, _ = yield from coarse_round(0, rhs, None, False)
        for k in range(3):
            lifted = lift(k, coarse[k])
            set_x(k, lifted)
            if k == 1:
                dual_ref[:, part_cols] = lifted
        if p == 0:
            send_n.wait()
            send_d.start()
        residual = res3[p, 1] - product(n_left, n_right)
        res3[p, 1] = residual

        coarse_res, _ = yield from coarse_round(1, residual, None, True)
        res3[p, 0] = r_recv[p, 1, 0].astype(f32)
        res3[p, 2] = r_recv[p, 1, 1].astype(f32)
        rho_prev = None
        slot = 0
        for step in range(ITERS):
            for k in range(3):
                projected = res3[p, k] - lift(k, coarse_res[k])
                set_x(k, projected)
                if k == 1:
                    vec[p] = projected
            if step == 0 and p == 0:
                send_d.wait()
            precond = product(d_left, d_right)
            stat = fold(vec[p] * precond)
            vec[p] = precond
            coarse, rho = yield from coarse_round(slot, precond, stat, True)
            for k in range(3):
                own = vec[p] if k == 1 else r_recv[p, slot, k // 2].astype(f32)
                direction = own - lift(k, coarse[k])
                if step > 0:
                    direction = direction + rho / rho_prev * dir3[p, k]
                dir3[p, k] = direction
                set_x(k, direction)
            slot = 1 - slot
            image = product(n_left, n_right)
            vec[p] = image
            stat = fold(dir3[p, 1] * image)
            if step + 1 < ITERS:
                coarse, curvature = yield from coarse_round(slot, image, stat, True)
                alpha = rho / curvature
                coarse_res = [old - alpha * new for old, new in zip(coarse_res, coarse)]
                res3[p, 0] = res3[p, 0] - alpha * r_recv[p, slot, 0].astype(f32)
                res3[p, 2] = res3[p, 2] - alpha * r_recv[p, slot, 1].astype(f32)
                res3[p, 1] = res3[p, 1] - alpha * vec[p]
                dual_ref[:, part_cols] = dual_ref[:, part_cols] + alpha * dir3[p, 1]
            else:
                gath[p, slot, s, waves:, :] = stat
                yield from exchange(slot, waves, STAT)
                group_stat = jnp.sum(gath[p, slot, :, waves:, :], axis=0)
                for h in range(groups):
                    stage[p, h, span:, :] = group_stat
                total = yield from reduce_groups(slot, span, STAT)
                alpha = rho / jnp.sum(total, axis=0, keepdims=True)
                dual_ref[:, part_cols] = dual_ref[:, part_cols] + alpha * dir3[p, 1]
                res_ref[:, part_cols] = res3[p, 1] - alpha * vec[p]
            slot = 1 - slot
            rho_prev = rho

    pipes = [pipeline(p) for p in range(PIPES)]
    send_u.wait_recv()
    for pipe in pipes:
        next(pipe)

    for copy in send_t:
        copy.wait()
    for h in range(groups):
        for k, source in enumerate((tile_nb.at[0], tile, tile_nb.at[1])):
            hi, lo = split(source[h * waves : (h + 1) * waves, :])
            tile_hi[h * span + k * waves : h * span + (k + 1) * waves, :] = hi
            tile_lo[h * span + k * waves : h * span + (k + 1) * waves, :] = lo
    load_d.wait()
    prepare(dirichlet, d_left, d_send)
    d_left[:, reach:] = dot(d_left[:, reach:], flip).astype(bf16)
    for copy in send_w:
        copy.wait()
    for k in range(3):
        stack_waves(k)

    while pipes:
        for pipe in list(pipes):
            try:
                next(pipe)
            except StopIteration:
                pipes.remove(pipe)


def shards(neumann, dirichlet, coarse_inverse, loads, iface_sizes, wave_dirs):
    width = neumann.shape[2]
    reach = width // 2
    columns = loads.shape[3]
    waves = wave_dirs.shape[2]
    groups, members = lax.axis_size("grp"), lax.axis_size("sub")
    rows, depth = coarse_inverse.shape[2:]
    span = 3 * waves
    cols = columns // PIPES
    vmem = pl.BlockSpec(memory_space=pltpu.VMEM)
    dma = pltpu.SemaphoreType.DMA
    vector = jax.ShapeDtypeStruct((reach, columns), f32)
    half_matrix = pltpu.VMEM((reach, width), bf16)
    dual, residual = pl.pallas_call(
        functools.partial(kernel, groups, members),
        out_shape=(vector, vector),
        in_specs=[
            pl.BlockSpec(memory_space=pltpu.SMEM), vmem, vmem, pl.BlockSpec(memory_space=pl.ANY), vmem, vmem,
        ],
        out_specs=(vmem, vmem),
        scratch_shapes=[
            pltpu.VMEM((width, width), bf16),
            half_matrix, half_matrix, half_matrix, half_matrix, half_matrix, half_matrix,
            pltpu.VMEM((reach, columns), f32),
            pltpu.VMEM((reach, columns), f32),
            pltpu.VMEM((2, rows, depth), f32),
            pltpu.VMEM((groups * span, depth), bf16),
            pltpu.VMEM((groups * span, depth), bf16),
            pltpu.VMEM((3, waves, reach), f32),
            pltpu.VMEM((3, reach, pl.cdiv(span, 128) * 128), bf16),
            pltpu.VMEM((2 * waves, reach), bf16),
            pltpu.VMEM((PIPES, 2, members, waves + STAT, cols), f32),
            pltpu.VMEM((PIPES, groups, span + STAT, cols), f32),
            pltpu.VMEM((PIPES, 2, groups, span + STAT, cols), f32),
            pltpu.VMEM((PIPES, 2, reach, cols), bf16),
            pltpu.VMEM((PIPES, 2, 2, reach, cols), bf16),
            pltpu.VMEM((PIPES, 3, reach, cols), f32),
            pltpu.VMEM((PIPES, 3, reach, cols), f32),
            pltpu.VMEM((PIPES, reach, cols), f32),
            pltpu.VMEM((reach, columns), f32),
            pltpu.VMEM((PIPES, width, cols), bf16),
            pltpu.VMEM((PIPES, width, cols), bf16),
            dma,
            dma((7,)),
            dma((7,)),
            dma((PIPES, 2, members // 2)),
            dma((PIPES, 2, members // 2)),
            dma((PIPES, 2, members)),
            dma((PIPES, 2, groups)),
            dma((PIPES, 2, groups)),
            dma((PIPES, 2, 2)),
            dma((PIPES, 2, 2)),
        ],
        compiler_params=pltpu.CompilerParams(
            collective_id=0, has_side_effects=True, vmem_limit_bytes=56 * 1024 * 1024
        ),
        cost_estimate=pl.CostEstimate(
            flops=14 * width * width * columns, bytes_accessed=5 * width * width, transcendentals=0
        ),
        name="dual_iterations",
    )(iface_sizes, wave_dirs[0], neumann[0, 0], dirichlet[0, 0], loads[0, 0], coarse_inverse[0, 0])
    return (dual[None, None], residual[None, None])


def solution(mesh):
    return jax.shard_map(
        shards,
        mesh=mesh,
        in_specs=(
            P("grp", "sub", None, None),
            P("grp", "sub", None, None),
            P("grp", "sub", None, None),
            P("grp", "sub", None, None),
            P("grp", "sub"),
            P("grp", "sub", None),
        ),
        out_specs=(P("grp", "sub", None, None), P("grp", "sub", None, None)),
        check_vma=False,
    )
```

```python
import functools

import jax
import jax.numpy as jnp
from jax import lax
from jax.experimental import pallas as pl
from jax.experimental.pallas import tpu as pltpu
from jax.sharding import PartitionSpec as P

NDIR = 64
ITERS = 2
WAVE_NUMBER = 0.785
STAT = 8
PIPES = 2
MESH = pl.DeviceIdType.MESH
f32, bf16 = jnp.float32, jnp.bfloat16


def dot(a, b):
    return jnp.dot(a, b, preferred_element_type=f32)


def split(values):
    high = values.astype(bf16)
    return high, (values - high.astype(f32)).astype(bf16)


def kernel(
    groups, members, size_ref, dirs_ref, neumann, dirichlet_hbm, loads, tile,
    dual_ref, res_ref,
    dirichlet, n_left, n_right, d_left, d_right, n_send, d_send,
    u_send, u_recv, tile_nb, tile_hi, tile_lo, bases, wave_cat, wave_t,
    gath, stage, red, r_send, r_recv,
    res3, dir3, vec, first, x_left, x_right,
    load_sem, set_send, set_recv, g_send, g_recv, red_send, red_recv, r_ssem, r_rsem,
):
    reach = n_left.shape[0]
    columns = loads.shape[1]
    waves = dirs_ref.shape[1]
    span = 3 * waves
    g, s = lax.axis_index("grp"), lax.axis_index("sub")
    nxt, prv = lax.rem(s + 1, members), lax.rem(s + members - 1, members)

    def remote(src, dst, send, recv, to):
        return pltpu.make_async_remote_copy(
            src_ref=src, dst_ref=dst, send_sem=send, recv_sem=recv, device_id=to, device_id_type=MESH
        )

    load_d = pltpu.make_async_copy(dirichlet_hbm, dirichlet, load_sem)
    load_d.start()

    barrier = pltpu.get_barrier_semaphore()

    def greet_sub(k, carry):
        pl.semaphore_signal(barrier, inc=1, device_id=(g, lax.rem(s + k, members)), device_id_type=MESH)
        return carry

    lax.fori_loop(1, members, greet_sub, 0)
    for k in range(1, groups):
        pl.semaphore_signal(barrier, inc=1, device_id=(lax.rem(g + k, groups), s), device_id_type=MESH)

    u_send[...] = dot(neumann[:reach, :], loads[...])
    pl.semaphore_wait(barrier, members - 1 + groups - 1)
    send_u = remote(u_send, u_recv, set_send.at[0], set_recv.at[0], (g, prv))
    send_u.start()
    send_t = [
        remote(tile, tile_nb.at[0], set_send.at[1], set_recv.at[1], (g, nxt)),
        remote(tile, tile_nb.at[1], set_send.at[2], set_recv.at[2], (g, prv)),
    ]

    back = (
        lax.broadcasted_iota(jnp.int32, (reach, reach), 0) + lax.broadcasted_iota(jnp.int32, (reach, reach), 1)
        == reach - 1
    )
    flip = jnp.where(back, 1.0, 0.0).astype(bf16)

    def prepare(matrix, left, outgoing):
        outgoing[:, :reach] = matrix[:reach, :reach]
        outgoing[:, reach:] = dot(matrix[:reach, reach:], flip).astype(bf16)
        left[...] = dot(flip, matrix[reach:, :]).astype(bf16)

    prepare(neumann, n_left, n_send)
    v = dot(n_left[...], loads[...])
    first[...] = v
    n_left[:, reach:] = dot(n_left[:, reach:], flip).astype(bf16)

    size = size_ref[0, 0]
    rows = lax.broadcasted_iota(jnp.int32, (waves, reach), 1)
    same = (
        lax.broadcasted_iota(jnp.int32, (waves, waves), 0) == lax.broadcasted_iota(jnp.int32, (waves, waves), 1)
    )
    dirs = jnp.sum(jnp.where(same, dirs_ref[...].astype(f32), 0.0), axis=1, keepdims=True)
    angle = 2.0 * jnp.pi * dirs / NDIR
    odd = lax.rem(lax.broadcasted_iota(jnp.int32, (waves, 1), 0), 2).astype(f32)
    basis = jnp.cos(WAVE_NUMBER * rows.astype(f32) * jnp.cos(angle) + odd * (jnp.pi / 2.0))
    basis = jnp.where(rows < size, basis, 0.0) / jnp.sqrt(f32(reach))
    high, low = split(basis)
    wave_t[:waves, :] = high
    wave_t[waves:, :] = low
    bases[1] = basis

    def stack_waves(k):
        hi, lo = split(bases[k])
        fill = jnp.zeros((wave_cat.shape[2] - span, reach), f32)
        padded = jnp.concatenate([hi.astype(f32), lo.astype(f32), hi.astype(f32), fill], axis=0)
        wave_cat[k] = padded.T.astype(bf16)

    send_w = [
        remote(bases.at[1], bases.at[0], set_send.at[3], set_recv.at[3], (g, nxt)),
        remote(bases.at[1], bases.at[2], set_send.at[4], set_recv.at[4], (g, prv)),
    ]
    send_n = remote(n_send, n_right, set_send.at[5], set_recv.at[5], (g, prv))
    send_d = remote(d_send, d_right, set_send.at[6], set_recv.at[6], (g, prv))
    send_u.wait_send()
    for copy in send_t + send_w + [send_n]:
        copy.start()

    cols = columns // PIPES
    live = lax.broadcasted_iota(jnp.int32, (reach, cols), 0) < size

    def lift(k, coarse):
        hi, lo = split(coarse)
        fill = jnp.zeros((wave_cat.shape[2] - span, cols), bf16)
        return dot(wave_cat[k], jnp.concatenate([hi, hi, lo, fill], axis=0))

    def fold(values):
        return jnp.sum(values.reshape(reach // STAT, STAT, cols), axis=0)

    def loop(body):
        def step(k, carry):
            body(k)
            return carry

        lax.fori_loop(1, members, step, 0, unroll=members <= 8)

    def pipeline(p):
        part_cols = slice(p * cols, (p + 1) * cols)

        def product(left, right):
            return jnp.where(live, dot(left[...], x_left[p]) + dot(right[...], x_right[p]), 0.0)

        def set_x(k, values):
            if k == 0:
                x_left[p, :reach, :] = (-values).astype(bf16)
            elif k == 1:
                own = values.astype(bf16)
                x_left[p, reach:, :] = own
                x_right[p, :reach, :] = own
            else:
                x_right[p, reach:, :] = (-values).astype(bf16)

        def exchange(slot, lo, count):
            part = pl.ds(lo, count)

            def block(owner):
                return gath.at[p, slot, owner, part]

            def send_peer(k):
                to = lax.rem(s + k, members)
                return remote(block(s), block(s), g_send.at[p, slot, k], g_recv.at[p, slot, s], (g, to))

            def arrival(k):
                src = lax.rem(s + members - k, members)
                return remote(block(src), block(src), g_send.at[p, slot, k], g_recv.at[p, slot, src], (g, nxt))

            loop(lambda k: send_peer(k).start())
            yield
            loop(lambda k: arrival(k).wait_recv())
            loop(lambda k: send_peer(k).wait_send())

        def reduce_groups(slot, lo, count):
            part = pl.ds(lo, count)

            def message(k, h, origin):
                return remote(
                    stage.at[p, h, part], red.at[p, slot, origin, part],
                    red_send.at[p, slot, k], red_recv.at[p, slot, origin], (h, s),
                )

            out = [message(k, lax.rem(g + k, groups), g) for k in range(1, groups)]
            into = [lax.rem(g + groups - k, groups) for k in range(1, groups)]
            for copy in out:
                copy.start()
            red[p, slot, g, part] = stage[p, g, part]
            yield
            for k, h in enumerate(into):
                message(k + 1, h, h).wait_recv()
            for copy in out:
                copy.wait_send()
            return jnp.sum(red[p, slot, :, part, :], axis=0)

        def send_rows(slot):
            return [
                remote(r_send.at[p, slot], r_recv.at[p, slot, side], r_ssem.at[p, slot, side],
                       r_rsem.at[p, slot, side], (g, to))
                for side, to in enumerate((nxt, prv))
            ]

        def coarse_round(slot, values, stat, share):
            hi, lo = split(values)
            both = dot(wave_t[...], hi)
            gath[p, slot, s, :waves, :] = both[:waves] + both[waves:] + dot(wave_t[:waves, :], lo)
            gath[p, slot, s, waves:, :] = jnp.zeros((STAT, cols), f32) if stat is None else stat
            if share:
                r_send[p, slot] = hi
            yield from exchange(slot, 0, waves + STAT)
            if share:
                for copy in send_rows(slot):
                    copy.start()
            blocks = gath[p, slot]
            c_hi, c_lo = split(blocks[:, :waves, :].reshape(members * waves, cols))
            terms = dot(tile_hi[...], c_hi) + dot(tile_lo[...], c_hi) + dot(tile_hi[...], c_lo)
            group_stat = jnp.sum(blocks[:, waves:, :], axis=0)
            for h in range(groups):
                stage[p, h, :span, :] = terms[h * span : (h + 1) * span]
                stage[p, h, span:, :] = group_stat
            total = yield from reduce_groups(slot, 0, span + STAT)
            if share:
                for copy in send_rows(slot):
                    copy.wait()
            coarse = [total[k * waves : (k + 1) * waves] for k in range(3)]
            return coarse, jnp.sum(total[span:], axis=0, keepdims=True)

        rhs = jnp.where(live, first[:, part_cols] - u_recv[:, part_cols], 0.0)
        res3[p, 1] = rhs
        coarse, _ = yield from coarse_round(0, rhs, None, False)
        for k in range(3):
            lifted = lift(k, coarse[k])
            set_x(k, lifted)
            if k == 1:
                dual_ref[:, part_cols] = lifted
        if p == 0:
            send_n.wait()
            send_d.start()
        residual = res3[p, 1] - product(n_left, n_right)
        res3[p, 1] = residual

        coarse_res, _ = yield from coarse_round(1, residual, None, True)
        res3[p, 0] = r_recv[p, 1, 0].astype(f32)
        res3[p, 2] = r_recv[p, 1, 1].astype(f32)
        rho_prev = None
        slot = 0
        for step in range(ITERS):
            for k in range(3):
                projected = res3[p, k] - lift(k, coarse_res[k])
                set_x(k, projected)
                if k == 1:
                    vec[p] = projected
            if step == 0 and p == 0:
                send_d.wait()
            precond = product(d_left, d_right)
            stat = fold(vec[p] * precond)
            vec[p] = precond
            coarse, rho = yield from coarse_round(slot, precond, stat, True)
            for k in range(3):
                own = vec[p] if k == 1 else r_recv[p, slot, k // 2].astype(f32)
                direction = own - lift(k, coarse[k])
                if step > 0:
                    direction = direction + rho / rho_prev * dir3[p, k]
                dir3[p, k] = direction
                set_x(k, direction)
            slot = 1 - slot
            image = product(n_left, n_right)
            vec[p] = image
            stat = fold(dir3[p, 1] * image)
            if step + 1 < ITERS:
                coarse, curvature = yield from coarse_round(slot, image, stat, True)
                alpha = rho / curvature
                coarse_res = [old - alpha * new for old, new in zip(coarse_res, coarse)]
                res3[p, 0] = res3[p, 0] - alpha * r_recv[p, slot, 0].astype(f32)
                res3[p, 2] = res3[p, 2] - alpha * r_recv[p, slot, 1].astype(f32)
                res3[p, 1] = res3[p, 1] - alpha * vec[p]
                dual_ref[:, part_cols] = dual_ref[:, part_cols] + alpha * dir3[p, 1]
            else:
                gath[p, slot, s, waves:, :] = stat
                yield from exchange(slot, waves, STAT)
                group_stat = jnp.sum(gath[p, slot, :, waves:, :], axis=0)
                for h in range(groups):
                    stage[p, h, span:, :] = group_stat
                total = yield from reduce_groups(slot, span, STAT)
                alpha = rho / jnp.sum(total, axis=0, keepdims=True)
                dual_ref[:, part_cols] = dual_ref[:, part_cols] + alpha * dir3[p, 1]
                res_ref[:, part_cols] = res3[p, 1] - alpha * vec[p]
            slot = 1 - slot
            rho_prev = rho

    pipes = [pipeline(p) for p in range(PIPES)]
    send_u.wait_recv()
    for pipe in pipes:
        next(pipe)

    for copy in send_t:
        copy.wait()
    for h in range(groups):
        for k, source in enumerate((tile_nb.at[0], tile, tile_nb.at[1])):
            hi, lo = split(source[h * waves : (h + 1) * waves, :])
            tile_hi[h * span + k * waves : h * span + (k + 1) * waves, :] = hi
            tile_lo[h * span + k * waves : h * span + (k + 1) * waves, :] = lo
    load_d.wait()
    prepare(dirichlet, d_left, d_send)
    d_left[:, reach:] = dot(d_left[:, reach:], flip).astype(bf16)
    for copy in send_w:
        copy.wait()
    for k in range(3):
        stack_waves(k)

    while pipes:
        for pipe in list(pipes):
            try:
                next(pipe)
            except StopIteration:
                pipes.remove(pipe)


def shards(neumann, dirichlet, coarse_inverse, loads, iface_sizes, wave_dirs):
    width = neumann.shape[2]
    reach = width // 2
    columns = loads.shape[3]
    waves = wave_dirs.shape[2]
    groups, members = lax.axis_size("grp"), lax.axis_size("sub")
    rows, depth = coarse_inverse.shape[2:]
    span = 3 * waves
    cols = columns // PIPES
    vmem = pl.BlockSpec(memory_space=pltpu.VMEM)
    dma = pltpu.SemaphoreType.DMA
    vector = jax.ShapeDtypeStruct((reach, columns), f32)
    half_matrix = pltpu.VMEM((reach, width), bf16)
    dual, residual = pl.pallas_call(
        functools.partial(kernel, groups, members),
        out_shape=(vector, vector),
        in_specs=[
            pl.BlockSpec(memory_space=pltpu.SMEM), vmem, vmem, pl.BlockSpec(memory_space=pl.ANY), vmem, vmem,
        ],
        out_specs=(vmem, vmem),
        scratch_shapes=[
            pltpu.VMEM((width, width), bf16),
            half_matrix, half_matrix, half_matrix, half_matrix, half_matrix, half_matrix,
            pltpu.VMEM((reach, columns), f32),
            pltpu.VMEM((reach, columns), f32),
            pltpu.VMEM((2, rows, depth), f32),
            pltpu.VMEM((groups * span, depth), bf16),
            pltpu.VMEM((groups * span, depth), bf16),
            pltpu.VMEM((3, waves, reach), f32),
            pltpu.VMEM((3, reach, pl.cdiv(span, 128) * 128), bf16),
            pltpu.VMEM((2 * waves, reach), bf16),
            pltpu.VMEM((PIPES, 2, members, waves + STAT, cols), f32),
            pltpu.VMEM((PIPES, groups, span + STAT, cols), f32),
            pltpu.VMEM((PIPES, 2, groups, span + STAT, cols), f32),
            pltpu.VMEM((PIPES, 2, reach, cols), bf16),
            pltpu.VMEM((PIPES, 2, 2, reach, cols), bf16),
            pltpu.VMEM((PIPES, 3, reach, cols), f32),
            pltpu.VMEM((PIPES, 3, reach, cols), f32),
            pltpu.VMEM((PIPES, reach, cols), f32),
            pltpu.VMEM((reach, columns), f32),
            pltpu.VMEM((PIPES, width, cols), bf16),
            pltpu.VMEM((PIPES, width, cols), bf16),
            dma,
            dma((7,)),
            dma((7,)),
            dma((PIPES, 2, members)),
            dma((PIPES, 2, members)),
            dma((PIPES, 2, groups)),
            dma((PIPES, 2, groups)),
            dma((PIPES, 2, 2)),
            dma((PIPES, 2, 2)),
        ],
        compiler_params=pltpu.CompilerParams(
            collective_id=0, has_side_effects=True, vmem_limit_bytes=56 * 1024 * 1024
        ),
        cost_estimate=pl.CostEstimate(
            flops=14 * width * width * columns, bytes_accessed=5 * width * width, transcendentals=0
        ),
        name="dual_iterations",
    )(iface_sizes, wave_dirs[0], neumann[0, 0], dirichlet[0, 0], loads[0, 0], coarse_inverse[0, 0])
    return (dual[None, None], residual[None, None])


def solution(mesh):
    return jax.shard_map(
        shards,
        mesh=mesh,
        in_specs=(
            P("grp", "sub", None, None),
            P("grp", "sub", None, None),
            P("grp", "sub", None, None),
            P("grp", "sub", None, None),
            P("grp", "sub"),
            P("grp", "sub", None),
        ),
        out_specs=(P("grp", "sub", None, None), P("grp", "sub", None, None)),
        check_vma=False,
    )
```

```python
import functools

import jax
import jax.numpy as jnp
from jax import lax
from jax.experimental import pallas as pl
from jax.experimental.pallas import tpu as pltpu
from jax.sharding import PartitionSpec as P

NDIR = 64
ITERS = 2
WAVE_NUMBER = 0.785
STAT = 8
PIPES = 2
MESH = pl.DeviceIdType.MESH
f32, bf16 = jnp.float32, jnp.bfloat16


def dot(a, b):
    return jnp.dot(a, b, preferred_element_type=f32)


def split(values):
    high = values.astype(bf16)
    return high, (values - high.astype(f32)).astype(bf16)


def kernel(
    groups, members, size_ref, dirs_ref, neumann, dirichlet_hbm, loads, tile,
    dual_ref, res_ref,
    dirichlet, n_left, n_right, d_left, d_right, n_send, d_send,
    u_send, u_recv, tile_nb, tile_hi, tile_lo, bases, wave_cat, wave_t,
    gath, stage, red, side_stage, side_red, r_send, r_recv,
    res3, dir3, vec, first, x_left, x_right,
    load_sem, set_send, set_recv, g_send, f_send, g_recv, red_send, red_recv, side_send, side_recv, s_send, r_ssem, r_rsem,
):
    reach = n_left.shape[0]
    columns = loads.shape[1]
    waves = dirs_ref.shape[1]
    span = 3 * waves
    half = members // 2
    g, s = lax.axis_index("grp"), lax.axis_index("sub")
    nxt, prv = lax.rem(s + 1, members), lax.rem(s + members - 1, members)
    partner = s + 1 - 2 * lax.rem(s, 2)

    def remote(src, dst, send, recv, to):
        return pltpu.make_async_remote_copy(
            src_ref=src, dst_ref=dst, send_sem=send, recv_sem=recv, device_id=to, device_id_type=MESH
        )

    load_d = pltpu.make_async_copy(dirichlet_hbm, dirichlet, load_sem)
    load_d.start()

    barrier = pltpu.get_barrier_semaphore()

    def greet_sub(k, carry):
        pl.semaphore_signal(barrier, inc=1, device_id=(g, lax.rem(s + k, members)), device_id_type=MESH)
        return carry

    lax.fori_loop(1, members, greet_sub, 0)
    for k in range(1, groups):
        pl.semaphore_signal(barrier, inc=1, device_id=(lax.rem(g + k, groups), s), device_id_type=MESH)

    u_send[...] = dot(neumann[:reach, :], loads[...])
    pl.semaphore_wait(barrier, members - 1 + groups - 1)
    send_u = remote(u_send, u_recv, set_send.at[0], set_recv.at[0], (g, prv))
    send_u.start()
    send_t = [
        remote(tile, tile_nb.at[0], set_send.at[1], set_recv.at[1], (g, nxt)),
        remote(tile, tile_nb.at[1], set_send.at[2], set_recv.at[2], (g, prv)),
    ]

    back = (
        lax.broadcasted_iota(jnp.int32, (reach, reach), 0) + lax.broadcasted_iota(jnp.int32, (reach, reach), 1)
        == reach - 1
    )
    flip = jnp.where(back, 1.0, 0.0).astype(bf16)

    def prepare(matrix, left, outgoing):
        outgoing[:, :reach] = matrix[:reach, :reach]
        outgoing[:, reach:] = dot(matrix[:reach, reach:], flip).astype(bf16)
        left[...] = dot(flip, matrix[reach:, :]).astype(bf16)

    prepare(neumann, n_left, n_send)
    v = dot(n_left[...], loads[...])
    first[...] = v
    n_left[:, reach:] = dot(n_left[:, reach:], flip).astype(bf16)

    size = size_ref[0, 0]
    rows = lax.broadcasted_iota(jnp.int32, (waves, reach), 1)
    same = (
        lax.broadcasted_iota(jnp.int32, (waves, waves), 0) == lax.broadcasted_iota(jnp.int32, (waves, waves), 1)
    )
    dirs = jnp.sum(jnp.where(same, dirs_ref[...].astype(f32), 0.0), axis=1, keepdims=True)
    angle = 2.0 * jnp.pi * dirs / NDIR
    odd = lax.rem(lax.broadcasted_iota(jnp.int32, (waves, 1), 0), 2).astype(f32)
    basis = jnp.cos(WAVE_NUMBER * rows.astype(f32) * jnp.cos(angle) + odd * (jnp.pi / 2.0))
    basis = jnp.where(rows < size, basis, 0.0) / jnp.sqrt(f32(reach))
    high, low = split(basis)
    wave_t[:waves, :] = high
    wave_t[waves:, :] = low
    bases[1] = basis

    def stack_waves(k):
        hi, lo = split(bases[k])
        fill = jnp.zeros((wave_cat.shape[2] - span, reach), f32)
        padded = jnp.concatenate([hi.astype(f32), lo.astype(f32), hi.astype(f32), fill], axis=0)
        wave_cat[k] = padded.T.astype(bf16)

    send_w = [
        remote(bases.at[1], bases.at[0], set_send.at[3], set_recv.at[3], (g, nxt)),
        remote(bases.at[1], bases.at[2], set_send.at[4], set_recv.at[4], (g, prv)),
    ]
    send_n = remote(n_send, n_right, set_send.at[5], set_recv.at[5], (g, prv))
    send_d = remote(d_send, d_right, set_send.at[6], set_recv.at[6], (g, prv))
    send_u.wait_send()
    for copy in send_t + send_w + [send_n]:
        copy.start()

    cols = columns // PIPES
    live = lax.broadcasted_iota(jnp.int32, (reach, cols), 0) < size

    def lift(k, coarse):
        hi, lo = split(coarse)
        fill = jnp.zeros((wave_cat.shape[2] - span, cols), bf16)
        return dot(wave_cat[k], jnp.concatenate([hi, hi, lo, fill], axis=0))

    def fold(values):
        return jnp.sum(values.reshape(reach // STAT, STAT, cols), axis=0)

    def loop(low, body):
        def step(k, carry):
            body(k)
            return carry

        lax.fori_loop(low, half, step, 0, unroll=half <= 8)

    def pipeline(p):
        part_cols = slice(p * cols, (p + 1) * cols)

        def product(left, right):
            return jnp.where(live, dot(left[...], x_left[p]) + dot(right[...], x_right[p]), 0.0)

        def set_x(k, values):
            if k == 0:
                x_left[p, :reach, :] = (-values).astype(bf16)
            elif k == 1:
                own = values.astype(bf16)
                x_left[p, reach:, :] = own
                x_right[p, :reach, :] = own
            else:
                x_right[p, reach:, :] = (-values).astype(bf16)

        def exchange(slot, lo, count):
            part = pl.ds(lo, count)

            def block(owner):
                return gath.at[p, slot, owner, part]

            def send_peer(k):
                to = lax.rem(s + 2 * k, members)
                return remote(block(s), block(s), g_send.at[p, slot, k], g_recv.at[p, slot, s], (g, to))

            def relay(k):
                src = lax.rem(s + members - 2 * k, members)
                return remote(block(src), block(src), f_send.at[p, slot, k], g_recv.at[p, slot, src], (g, partner))

            def arrival(k):
                src = lax.rem(partner + members - 2 * k, members)
                return remote(block(src), block(src), f_send.at[p, slot, k], g_recv.at[p, slot, src], (g, partner))

            loop(1, lambda k: send_peer(k).start())
            relay(0).start()
            yield

            def pass_on(k):
                relay(k).wait_recv()
                relay(k).start()

            loop(1, pass_on)
            loop(0, lambda k: arrival(k).wait_recv())
            loop(1, lambda k: send_peer(k).wait_send())
            loop(0, lambda k: relay(k).wait_send())

        def exchange_small(slot, lo, count):
            part = pl.ds(lo, count)

            def send(k):
                to, ours = lax.rem(s + k, members), gath.at[p, slot, s, part]
                return remote(ours, ours, s_send.at[p, k], g_recv.at[p, slot, s], (g, to))

            def arrival(k):
                src = lax.rem(s + members - k, members)
                theirs = gath.at[p, slot, src, part]
                return remote(theirs, theirs, s_send.at[p, k], g_recv.at[p, slot, src], (g, nxt))

            def each(body):
                def step(k, carry):
                    body(k)
                    return carry

                lax.fori_loop(1, members, step, 0, unroll=members <= 8)

            each(lambda k: send(k).start())
            yield
            each(lambda k: arrival(k).wait_recv())
            each(lambda k: send(k).wait_send())

        def reduce_groups(slot, lo, count, sides):
            part = pl.ds(lo, count)

            def messages(k, h, origin):
                both = [
                    remote(
                        stage.at[p, h, part], red.at[p, slot, origin, part],
                        red_send.at[p, slot, k], red_recv.at[p, slot, origin], (h, s),
                    )
                ]
                if sides:
                    both.append(
                        remote(
                            side_stage.at[p, h], side_red.at[p, slot, origin],
                            side_send.at[p, slot, k], side_recv.at[p, slot, origin], (h, s),
                        )
                    )
                return both

            out = [copy for k in range(1, groups) for copy in messages(k, lax.rem(g + k, groups), g)]
            into = [lax.rem(g + groups - k, groups) for k in range(1, groups)]
            for copy in out:
                copy.start()
            red[p, slot, g, part] = stage[p, g, part]
            if sides:
                side_red[p, slot, g] = side_stage[p, g]
            yield
            for k, h in enumerate(into):
                for copy in messages(k + 1, h, h):
                    copy.wait_recv()
            for copy in out:
                copy.wait_send()
            total = jnp.sum(red[p, slot, :, part, :], axis=0)
            if not sides:
                return total
            return total, jnp.sum(side_red[p, slot].astype(f32), axis=0)

        def send_rows(slot):
            return [
                remote(r_send.at[p, slot], r_recv.at[p, slot, side], r_ssem.at[p, slot, side],
                       r_rsem.at[p, slot, side], (g, to))
                for side, to in enumerate((nxt, prv))
            ]

        def coarse_round(slot, values, stat, share):
            hi, lo = split(values)
            both = dot(wave_t[...], hi)
            gath[p, slot, s, :waves, :] = both[:waves] + both[waves:] + dot(wave_t[:waves, :], lo)
            used = waves if stat is None else waves + STAT
            if stat is not None:
                gath[p, slot, s, waves:, :] = stat
            if share:
                r_send[p, slot] = hi
            yield from exchange(slot, 0, used)
            if share:
                for copy in send_rows(slot):
                    copy.start()
            c_hi, c_lo = split(gath[p, slot, :, :waves, :].reshape(members * waves, cols))
            terms = dot(tile_hi[...], c_hi) + dot(tile_lo[...], c_hi) + dot(tile_hi[...], c_lo)
            group_stat = None if stat is None else jnp.sum(gath[p, slot, :, waves:, :], axis=0)
            for h in range(groups):
                rows = terms[h * span : (h + 1) * span]
                stage[p, h, :waves, :] = rows[waves : 2 * waves]
                side_stage[p, h, :waves, :] = rows[:waves].astype(bf16)
                side_stage[p, h, waves:, :] = rows[2 * waves :].astype(bf16)
                if stat is not None:
                    stage[p, h, waves:, :] = group_stat
            total, sides = yield from reduce_groups(slot, 0, used, True)
            if share:
                for copy in send_rows(slot):
                    copy.wait()
            coarse = [sides[:waves], total[:waves], sides[waves:]]
            return coarse, None if stat is None else jnp.sum(total[waves:], axis=0, keepdims=True)

        rhs = jnp.where(live, first[:, part_cols] - u_recv[:, part_cols], 0.0)
        res3[p, 1] = rhs
        coarse, _ = yield from coarse_round(0, rhs, None, False)
        for k in range(3):
            lifted = lift(k, coarse[k])
            set_x(k, lifted)
            if k == 1:
                dual_ref[:, part_cols] = lifted
        if p == 0:
            send_n.wait()
            send_d.start()
        residual = res3[p, 1] - product(n_left, n_right)
        res3[p, 1] = residual

        coarse_res, _ = yield from coarse_round(1, residual, None, True)
        res3[p, 0] = r_recv[p, 1, 0].astype(f32)
        res3[p, 2] = r_recv[p, 1, 1].astype(f32)
        rho_prev = None
        slot = 0
        for step in range(ITERS):
            for k in range(3):
                projected = res3[p, k] - lift(k, coarse_res[k])
                set_x(k, projected)
                if k == 1:
                    vec[p] = projected
            if step == 0 and p == 0:
                send_d.wait()
            precond = product(d_left, d_right)
            stat = fold(vec[p] * precond)
            vec[p] = precond
            coarse, rho = yield from coarse_round(slot, precond, stat, True)
            for k in range(3):
                own = vec[p] if k == 1 else r_recv[p, slot, k // 2].astype(f32)
                direction = own - lift(k, coarse[k])
                if step > 0:
                    direction = direction + rho / rho_prev * dir3[p, k]
                dir3[p, k] = direction
                set_x(k, direction)
            slot = 1 - slot
            image = product(n_left, n_right)
            vec[p] = image
            stat = fold(dir3[p, 1] * image)
            if step + 1 < ITERS:
                coarse, curvature = yield from coarse_round(slot, image, stat, True)
                alpha = rho / curvature
                coarse_res = [old - alpha * new for old, new in zip(coarse_res, coarse)]
                res3[p, 0] = res3[p, 0] - alpha * r_recv[p, slot, 0].astype(f32)
                res3[p, 2] = res3[p, 2] - alpha * r_recv[p, slot, 1].astype(f32)
                res3[p, 1] = res3[p, 1] - alpha * vec[p]
                dual_ref[:, part_cols] = dual_ref[:, part_cols] + alpha * dir3[p, 1]
            else:
                gath[p, slot, s, waves:, :] = stat
                yield from exchange_small(slot, waves, STAT)
                group_stat = jnp.sum(gath[p, slot, :, waves:, :], axis=0)
                for h in range(groups):
                    stage[p, h, waves:, :] = group_stat
                total = yield from reduce_groups(slot, waves, STAT, False)
                alpha = rho / jnp.sum(total, axis=0, keepdims=True)
                dual_ref[:, part_cols] = dual_ref[:, part_cols] + alpha * dir3[p, 1]
                res_ref[:, part_cols] = res3[p, 1] - alpha * vec[p]
            slot = 1 - slot
            rho_prev = rho

    pipes = [pipeline(p) for p in range(PIPES)]
    send_u.wait_recv()
    for pipe in pipes:
        next(pipe)

    for copy in send_t:
        copy.wait()
    for h in range(groups):
        for k, source in enumerate((tile_nb.at[0], tile, tile_nb.at[1])):
            hi, lo = split(source[h * waves : (h + 1) * waves, :])
            tile_hi[h * span + k * waves : h * span + (k + 1) * waves, :] = hi
            tile_lo[h * span + k * waves : h * span + (k + 1) * waves, :] = lo
    load_d.wait()
    prepare(dirichlet, d_left, d_send)
    d_left[:, reach:] = dot(d_left[:, reach:], flip).astype(bf16)
    for copy in send_w:
        copy.wait()
    for k in range(3):
        stack_waves(k)

    while pipes:
        for pipe in list(pipes):
            try:
                next(pipe)
            except StopIteration:
                pipes.remove(pipe)


def shards(neumann, dirichlet, coarse_inverse, loads, iface_sizes, wave_dirs):
    width = neumann.shape[2]
    reach = width // 2
    columns = loads.shape[3]
    waves = wave_dirs.shape[2]
    groups, members = lax.axis_size("grp"), lax.axis_size("sub")
    rows, depth = coarse_inverse.shape[2:]
    span = 3 * waves
    cols = columns // PIPES
    vmem = pl.BlockSpec(memory_space=pltpu.VMEM)
    dma = pltpu.SemaphoreType.DMA
    vector = jax.ShapeDtypeStruct((reach, columns), f32)
    half_matrix = pltpu.VMEM((reach, width), bf16)
    dual, residual = pl.pallas_call(
        functools.partial(kernel, groups, members),
        out_shape=(vector, vector),
        in_specs=[
            pl.BlockSpec(memory_space=pltpu.SMEM), vmem, vmem, pl.BlockSpec(memory_space=pl.ANY), vmem, vmem,
        ],
        out_specs=(vmem, vmem),
        scratch_shapes=[
            pltpu.VMEM((width, width), bf16),
            half_matrix, half_matrix, half_matrix, half_matrix, half_matrix, half_matrix,
            pltpu.VMEM((reach, columns), f32),
            pltpu.VMEM((reach, columns), f32),
            pltpu.VMEM((2, rows, depth), f32),
            pltpu.VMEM((groups * span, depth), bf16),
            pltpu.VMEM((groups * span, depth), bf16),
            pltpu.VMEM((3, waves, reach), f32),
            pltpu.VMEM((3, reach, pl.cdiv(span, 128) * 128), bf16),
            pltpu.VMEM((2 * waves, reach), bf16),
            pltpu.VMEM((PIPES, 2, members, waves + STAT, cols), f32),
            pltpu.VMEM((PIPES, groups, waves + STAT, cols), f32),
            pltpu.VMEM((PIPES, 2, groups, waves + STAT, cols), f32),
            pltpu.VMEM((PIPES, groups, 2 * waves, cols), bf16),
            pltpu.VMEM((PIPES, 2, groups, 2 * waves, cols), bf16),
            pltpu.VMEM((PIPES, 2, reach, cols), bf16),
            pltpu.VMEM((PIPES, 2, 2, reach, cols), bf16),
            pltpu.VMEM((PIPES, 3, reach, cols), f32),
            pltpu.VMEM((PIPES, 3, reach, cols), f32),
            pltpu.VMEM((PIPES, reach, cols), f32),
            pltpu.VMEM((reach, columns), f32),
            pltpu.VMEM((PIPES, width, cols), bf16),
            pltpu.VMEM((PIPES, width, cols), bf16),
            dma,
            dma((7,)),
            dma((7,)),
            dma((PIPES, 2, members // 2)),
            dma((PIPES, 2, members // 2)),
            dma((PIPES, 2, members)),
            dma((PIPES, 2, groups)),
            dma((PIPES, 2, groups)),
            dma((PIPES, 2, groups)),
            dma((PIPES, 2, groups)),
            dma((PIPES, members)),
            dma((PIPES, 2, 2)),
            dma((PIPES, 2, 2)),
        ],
        compiler_params=pltpu.CompilerParams(
            collective_id=0, has_side_effects=True, vmem_limit_bytes=56 * 1024 * 1024
        ),
        cost_estimate=pl.CostEstimate(
            flops=14 * width * width * columns, bytes_accessed=5 * width * width, transcendentals=0
        ),
        name="dual_iterations",
    )(iface_sizes, wave_dirs[0], neumann[0, 0], dirichlet[0, 0], loads[0, 0], coarse_inverse[0, 0])
    return (dual[None, None], residual[None, None])


def solution(mesh):
    return jax.shard_map(
        shards,
        mesh=mesh,
        in_specs=(
            P("grp", "sub", None, None),
            P("grp", "sub", None, None),
            P("grp", "sub", None, None),
            P("grp", "sub", None, None),
            P("grp", "sub"),
            P("grp", "sub", None),
        ),
        out_specs=(P("grp", "sub", None, None), P("grp", "sub", None, None)),
        check_vma=False,
    )
```
